32 devices in a mesh: groups: 2 (over y), ctx: 4 (over z), tp: 4 (over x, core).
Axes of the slice: x: 2, y: 2, z: 4, core: 2. Of those that a mesh axis runs over, the one named last changes fastest.
Arguments:
- queries: bfloat16 [2048, 64, 128], P(('groups', 'ctx'), 'tp'), parts along dimension 0, may hold values from -4.5 to 4.5
- keys: bfloat16 [2048, 8, 128], P(('groups', 'ctx'), 'tp'), parts along dimension 0, may hold values from -5.5 to 5.5
- values: bfloat16 [2048, 8, 128], P(('groups', 'ctx'), 'tp'), parts along dimension 0, may hold values from -6 to 6
- doc_pos: int32 [2048], P(('groups', 'ctx')), parts along dimension 0, may hold values from 0 to 511, as said below
- log_decay: float32 [2048, 64], P(('groups', 'ctx'), 'tp'), parts along dimension 0, may hold values from -0.8 to 0
- student_c: bfloat16 [2048, 64, 128], P(('groups', 'ctx'), 'tp'), parts along dimension 0, may hold values from -6 to 6
- student_write: bfloat16 [2048, 8, 128], P(('groups', 'ctx'), 'tp'), parts along dimension 0, may hold values from -6 to 6
- student_input: bfloat16 [2048, 8, 128], P(('groups', 'ctx'), 'tp'), parts along dimension 0, may hold values from -46 to 46
- gain: float32 [64, 128], P('tp'), may hold values from 0.5 to 1.5
Outputs:
- readout_gradient: bfloat16 [2048, 64, 128], P(('groups', 'ctx'), 'tp'), parts along dimension 0
- write_gradient: bfloat16 [2048, 8, 128], P(('groups', 'ctx'), 'tp'), parts along dimension 0
- input_gradient: bfloat16 [2048, 8, 128], P(('groups', 'ctx'), 'tp'), parts along dimension 0
- grad_gain: float32 [128, 128], P(('groups', 'tp')), parts along dimension 0
The draws below stay inside these ranges and needn't reach their ends.
There are 2 independent parts, one for each index of `groups`. The reference program is written for one: setup_inputs(seed, part) draws one part's arguments, and reference() takes and returns one part's arrays. A program takes and returns all parts, laid end to end along the dimension named above; an argument that names none is the same for every part. Nothing has to cross between parts.
Inputs may be any that keep to these rules, and one draw needn't show every extreme that they name: `doc_pos`: every document starts with position 0 and counts up by one a token; the first token starts a document; the longest document has exactly 512 tokens.
All inputs are finite; a program needn't handle non-finite values.
Results may differ from the reference program's by a relative error of at most 0.0075.
Values may be sent and summed in bfloat16 or wider, within the bound.
A program may use at most 128 MiB of HBM per device.

```python
import math
import jax
import jax.numpy as jnp
from jax import lax

ATTENTION_LANES = 64
KV_HEADS = 8
HEAD_SIZE = 128
STATE_SIZE = 128
TOKENS_PER_SHARD = 256
SEGMENT_SPAN = 1024
DOC_MOST = 512
N_CTX = 4


def bulk_values(key, shape):
    return jnp.clip(jax.random.normal(key, shape, jnp.float32), -4.5, 4.5)


def draw_queries(key, part):
    drawn_entries = bulk_values(jax.random.fold_in(key, 1), (SEGMENT_SPAN, ATTENTION_LANES, HEAD_SIZE))
    return drawn_entries.astype(jnp.bfloat16)


def draw_keys(key, part):
    drawn_entries = bulk_values(jax.random.fold_in(key, 2), (SEGMENT_SPAN, KV_HEADS, HEAD_SIZE))
    return drawn_entries.astype(jnp.bfloat16)


def draw_doc_pos(key, part):
    longest = SEGMENT_SPAN // 2
    big_start = jax.random.randint(jax.random.fold_in(key, 21), (), 0, SEGMENT_SPAN - longest + 1)
    cut_marks = jax.random.randint(jax.random.fold_in(key, 22), (SEGMENT_SPAN,), 0, TOKENS_PER_SHARD) == 0
    indices = jnp.arange(SEGMENT_SPAN, dtype=jnp.int32)
    inside = (indices > big_start) & (indices < big_start + longest)
    begins = (indices == 0) | (indices == big_start) | (indices == big_start + longest) | cut_marks & jnp.logical_not(inside)
    latest = lax.cummax(jnp.where(begins, indices, 0), axis=0)
    return (indices - latest).astype(jnp.int32)


def draw_log_decay(key, part):
    fast_share = 0.5
    fast_heads = jax.random.uniform(jax.random.fold_in(key, 31), (ATTENTION_LANES,)) < fast_share
    slow_rate = jax.random.uniform(jax.random.fold_in(key, 32), (ATTENTION_LANES,), jnp.float32, 0.3, 1.0) / SEGMENT_SPAN
    fast_rate = jax.random.uniform(jax.random.fold_in(key, 33), (ATTENTION_LANES,), jnp.float32, 1.0 / 50.0, 1.0 / 30.0)
    lane_forgetting_factor = jnp.where(fast_heads, fast_rate, slow_rate)
    rough_entries = jnp.exp(jax.random.uniform(jax.random.fold_in(key, 34), (SEGMENT_SPAN, ATTENTION_LANES), jnp.float32, math.log(0.5), math.log(2.0)))
    run_agreement = jax.random.uniform(jax.random.fold_in(key, 35), (SEGMENT_SPAN, ATTENTION_LANES)) < 2.0 / SEGMENT_SPAN
    run_extent = jnp.log(jax.random.uniform(jax.random.fold_in(key, 36), (SEGMENT_SPAN, ATTENTION_LANES), jnp.float32, 0.5, 0.8))
    drawn_entries = -lane_forgetting_factor[None, :] * rough_entries + jnp.where(run_agreement, run_extent, 0.0)
    return drawn_entries.astype(jnp.float32)


def draw_student_input(key, part):
    drawn_entries = bulk_values(jax.random.fold_in(key, 41), (SEGMENT_SPAN, KV_HEADS, HEAD_SIZE))
    column_scale = jnp.exp(jax.random.uniform(jax.random.fold_in(key, 43), (1, KV_HEADS, HEAD_SIZE), jnp.float32, 0.0, math.log(10.0))) / math.sqrt(10.0)
    row_scale = jnp.exp(jax.random.uniform(jax.random.fold_in(key, 44), (SEGMENT_SPAN, 1, 1), jnp.float32, 0.0, math.log(10.0))) / math.sqrt(10.0)
    return (drawn_entries * column_scale * row_scale).astype(jnp.bfloat16)


def shard_levels(own_key, extent, cuts, low, top_value):
    level, own = 1.0, jax.random.fold_in(own_key, 6)
    for position, parts in cuts:
        steps = jnp.exp(jax.random.uniform(jax.random.fold_in(own, position), (parts,), jnp.float32, low / len(cuts), top_value / len(cuts)))
        level = level * jnp.repeat(steps, extent[position] // parts).reshape([-1 if axis == position else 1 for axis in range(len(extent))])
    return level


def scatter_about(rng, extent, deviation, bound, split=(), kind=jnp.bfloat16):
    array = deviation * jax.random.normal(rng, extent, jnp.float32)
    if split:
        array = array * shard_levels(rng, extent, split, -0.22, 0.18)
    return jnp.clip(array, -bound, bound).astype(kind)


def setup_inputs(seed: int = 0, part: int = 0) -> dict:
    key_list = jax.random.split(jax.random.key(seed), 10)
    part_keys = jax.random.split(jax.random.fold_in(key_list[9], part), 10)
    queries = draw_queries(jax.random.fold_in(jax.random.fold_in(key_list[9], part), 71), part)
    keys = draw_keys(jax.random.fold_in(jax.random.fold_in(key_list[9], part), 71), part)
    values = scatter_about(part_keys[2], (SEGMENT_SPAN, KV_HEADS, HEAD_SIZE), 1.0, 6.0, ((0, 4), (1, 4)))
    doc_pos = draw_doc_pos(jax.random.fold_in(jax.random.fold_in(key_list[9], part), 71), part)
    log_decay = draw_log_decay(jax.random.fold_in(jax.random.fold_in(key_list[9], part), 71), part)
    student_c = scatter_about(part_keys[5], (SEGMENT_SPAN, ATTENTION_LANES, STATE_SIZE), 1.0, 6.0, ((0, 4), (1, 4)))
    student_write = scatter_about(part_keys[6], (SEGMENT_SPAN, KV_HEADS, STATE_SIZE), 1.0, 6.0, ((0, 4), (1, 4)))
    student_input = draw_student_input(jax.random.fold_in(jax.random.fold_in(key_list[9], part), 71), part)
    gain = jnp.clip(1.0 + 0.1 * jax.random.normal(key_list[8], (ATTENTION_LANES, HEAD_SIZE), jnp.float32), 0.5, 1.5)
    return {"queries": queries, "keys": keys, "values": values, "doc_pos": doc_pos, "log_decay": log_decay, "student_c": student_c, "student_write": student_write, "student_input": student_input, "gain": gain}


EPSILON = 1e-05
STUDENT_FLOOR = 1.0

def to_low(array_in):
    return lax.optimization_barrier(array_in.astype(jnp.bfloat16)).astype(jnp.float32)

def teacher_targets(queries, keys, values, doc_start):
    repeat = ATTENTION_LANES // KV_HEADS
    block_rows = math.gcd(SEGMENT_SPAN, 512)
    key_span = min(SEGMENT_SPAN, DOC_MOST + block_rows)
    score_scale = 1.0 / math.sqrt(HEAD_SIZE)

    def one_block(block_index):
        first_row = block_index * block_rows
        key_begin = jnp.clip(first_row + block_rows - key_span, 0, SEGMENT_SPAN - key_span).astype(jnp.int32)
        query_pos = first_row + jnp.arange(block_rows, dtype=jnp.int32)
        key_pos = key_begin + jnp.arange(key_span, dtype=jnp.int32)
        query_start = lax.dynamic_slice_in_dim(doc_start, first_row, block_rows, 0)
        visible = (key_pos[None, :] <= query_pos[:, None]) & (key_pos[None, :] >= query_start[:, None])
        query_block = lax.dynamic_slice_in_dim(queries, first_row, block_rows, 0).astype(jnp.float32)
        key_tile = lax.dynamic_slice_in_dim(keys, key_begin, key_span, 0).astype(jnp.float32)
        value_block = lax.dynamic_slice_in_dim(values, key_begin, key_span, 0).astype(jnp.float32)
        grouped_rows = query_block.reshape(block_rows, KV_HEADS, repeat, HEAD_SIZE)

        def one_group(group_index):
            group_query = lax.dynamic_index_in_dim(grouped_rows, group_index, 1, keepdims=False)
            group_key = lax.dynamic_index_in_dim(key_tile, group_index, 1, keepdims=False)
            group_value = lax.dynamic_index_in_dim(value_block, group_index, 1, keepdims=False)
            score_matrix = jnp.einsum('trd,sd->rts', group_query, group_key) * score_scale
            score_matrix = jnp.where(visible[None], score_matrix, -jnp.inf)
            row_top = lax.optimization_barrier(jnp.max(score_matrix, axis=-1, keepdims=True))
            weights = to_low(jnp.exp(score_matrix - row_top))
            mixed_out = jnp.einsum('rts,sd->trd', weights, group_value)
            normed = mixed_out / jnp.sqrt(lax.optimization_barrier(jnp.mean(mixed_out * mixed_out, axis=-1, keepdims=True)) + EPSILON)
            return normed.astype(jnp.bfloat16)
        per_group = lax.map(one_group, jnp.arange(KV_HEADS, dtype=jnp.int32))
        return per_group.transpose(1, 0, 2, 3).reshape(block_rows, ATTENTION_LANES, HEAD_SIZE)
    blocks = lax.map(one_block, jnp.arange(SEGMENT_SPAN // block_rows, dtype=jnp.int32))
    return blocks.reshape(SEGMENT_SPAN, ATTENTION_LANES, HEAD_SIZE)

def block_levels(block_index, doc_start, log_decay):
    first_row = block_index * TOKENS_PER_SHARD
    positions = first_row + jnp.arange(TOKENS_PER_SHARD, dtype=jnp.int32)
    starts = lax.dynamic_slice_in_dim(doc_start, first_row, TOKENS_PER_SHARD, 0)
    log_level = jnp.cumsum(lax.dynamic_slice_in_dim(log_decay, first_row, TOKENS_PER_SHARD, 0), axis=0)
    level_rows = log_level.T
    same_doc = (positions[None, :] <= positions[:, None]) & (positions[None, :] >= starts[:, None])
    fade = jnp.exp(jnp.where(same_doc[None], level_rows[:, :, None] - level_rows[:, None, :], -jnp.inf))
    last_start = starts[-1]
    tail_fade = jnp.where((positions >= last_start)[:, None], jnp.exp(log_level[-1:, :] - log_level), 0.0)
    block_decay = jnp.where(last_start < first_row, jnp.exp(log_level[-1]), 0.0)
    head_fade = jnp.where((starts < first_row)[:, None], jnp.exp(log_level), 0.0)
    return (fade, tail_fade, block_decay, head_fade)

def block_inputs(block_index, student_c, student_write, student_input):
    repeat = ATTENTION_LANES // KV_HEADS
    first_row = block_index * TOKENS_PER_SHARD
    readout_rows = lax.dynamic_slice_in_dim(student_c, first_row, TOKENS_PER_SHARD, 0).astype(jnp.float32)
    write_rows = lax.dynamic_slice_in_dim(student_write, first_row, TOKENS_PER_SHARD, 0).astype(jnp.float32)
    input_rows = lax.dynamic_slice_in_dim(student_input, first_row, TOKENS_PER_SHARD, 0).astype(jnp.float32)
    return (readout_rows.reshape(TOKENS_PER_SHARD, KV_HEADS, repeat, STATE_SIZE), write_rows, input_rows)

def end_state(block_index, doc_start, log_decay, student_c, student_write, student_input):
    repeat = ATTENTION_LANES // KV_HEADS
    fade, tail_fade, block_decay, head_fade = block_levels(block_index, doc_start, log_decay)
    readout_rows, write_rows, input_rows = block_inputs(block_index, student_c, student_write, student_input)
    scaled_b = to_low(tail_fade.reshape(TOKENS_PER_SHARD, KV_HEADS, repeat)[..., None] * write_rows[:, :, None, :])
    block_state = jnp.einsum('tgrn,tgp->grnp', scaled_b, input_rows).reshape(ATTENTION_LANES, STATE_SIZE, HEAD_SIZE)
    return (block_decay, block_state)

def forward_block(block_index, carry_state, doc_start, log_decay, student_c, student_write, student_input, gain, target):
    repeat = ATTENTION_LANES // KV_HEADS
    fade, tail_fade, block_decay, head_fade = block_levels(block_index, doc_start, log_decay)
    readout_rows, write_rows, input_rows = block_inputs(block_index, student_c, student_write, student_input)
    inner_product = jnp.einsum('oizy,eiy->izoe', readout_rows, write_rows).reshape(ATTENTION_LANES, TOKENS_PER_SHARD, TOKENS_PER_SHARD)
    decay_kernel = to_low(fade * inner_product).reshape(KV_HEADS, repeat, TOKENS_PER_SHARD, TOKENS_PER_SHARD)
    within_block = jnp.einsum('dlmx,xdc->mdlc', decay_kernel, input_rows).reshape(TOKENS_PER_SHARD, ATTENTION_LANES, HEAD_SIZE)
    carry_low = to_low(carry_state)
    from_carry = jnp.einsum('thn,hnp->thp', readout_rows.reshape(TOKENS_PER_SHARD, ATTENTION_LANES, STATE_SIZE), carry_low) * head_fade[..., None]
    mixer = within_block + from_carry
    root_mean = jnp.sqrt(lax.optimization_barrier(jnp.mean(mixer * mixer, axis=-1, keepdims=True)) + STUDENT_FLOOR)
    normed = mixer / root_mean
    target_rows = lax.dynamic_slice_in_dim(target, block_index * TOKENS_PER_SHARD, TOKENS_PER_SHARD, 0).astype(jnp.float32)
    residual_diff = normed * gain[None] - target_rows
    gain_term = lax.optimization_barrier(jnp.sum(residual_diff * normed, axis=0))
    scaled_diff = residual_diff * gain[None]
    mixer_grad = to_low((scaled_diff - normed * lax.optimization_barrier(jnp.mean(scaled_diff * normed, axis=-1, keepdims=True))) / root_mean)
    faded_c = to_low(head_fade[..., None] * readout_rows.reshape(TOKENS_PER_SHARD, ATTENTION_LANES, STATE_SIZE))
    back_state = jnp.einsum('thn,thp->hnp', faded_c, mixer_grad)
    return (fade, decay_kernel, readout_rows, write_rows, input_rows, tail_fade, head_fade, carry_low, mixer_grad, gain_term, back_state)

def reference(queries, keys, values, doc_pos, log_decay, student_c, student_write, student_input, gain):
    repeat = ATTENTION_LANES // KV_HEADS
    doc_start = jnp.arange(SEGMENT_SPAN, dtype=jnp.int32) - doc_pos
    target = teacher_targets(queries, keys, values, doc_start)
    block_ids = jnp.arange(N_CTX, dtype=jnp.int32)

    def ends_of(block_index):
        return end_state(block_index, doc_start, log_decay, student_c, student_write, student_input)
    decays, states = lax.map(ends_of, block_ids)

    def chain_step(running, inputs):
        decay_now, state_now = inputs
        return (decay_now[:, None, None] * running + state_now, running)
    empty = jnp.zeros((ATTENTION_LANES, STATE_SIZE, HEAD_SIZE), jnp.float32)
    _, carry_in = lax.scan(chain_step, empty, (decays, states))

    def backward_terms(inputs):
        block_index, carry_state = inputs
        pieces = forward_block(block_index, carry_state, doc_start, log_decay, student_c, student_write, student_input, gain, target)
        return (pieces[9], pieces[10])
    gain_terms, back_states = lax.map(backward_terms, (block_ids, carry_in))
    _, carry_back = lax.scan(chain_step, empty, (decays, back_states), reverse=True)

    def final_grads(inputs):
        block_index, carry_state, carry_grad = inputs
        pieces = forward_block(block_index, carry_state, doc_start, log_decay, student_c, student_write, student_input, gain, target)
        fade, decay_kernel, readout_rows, write_rows, input_rows, tail_fade, head_fade, carry_low, mixer_grad = pieces[:9]
        back_low = to_low(carry_grad)
        grouped_gradient = mixer_grad.reshape(TOKENS_PER_SHARD, KV_HEADS, repeat, HEAD_SIZE)
        gradient_product = jnp.einsum('zmhx,jmx->mhzj', grouped_gradient, input_rows).reshape(ATTENTION_LANES, TOKENS_PER_SHARD, TOKENS_PER_SHARD)
        kernel_gradient = to_low(fade * gradient_product).reshape(KV_HEADS, repeat, TOKENS_PER_SHARD, TOKENS_PER_SHARD)
        readout_gradient = jnp.einsum('cmdu,ucx->dcmx', kernel_gradient, write_rows).reshape(TOKENS_PER_SHARD, ATTENTION_LANES, STATE_SIZE)
        readout_gradient = readout_gradient + head_fade[..., None] * jnp.einsum('thp,hnp->thn', mixer_grad, carry_low)
        grouped_fade = tail_fade.reshape(TOKENS_PER_SHARD, KV_HEADS, repeat, 1)
        grouped_back = back_low.reshape(KV_HEADS, repeat, STATE_SIZE, HEAD_SIZE)
        write_gradient = jnp.einsum('uyzx,zuye->xue', kernel_gradient, readout_rows)
        write_gradient = write_gradient + lax.optimization_barrier(jnp.sum(grouped_fade * jnp.einsum('grnp,sgp->sgrn', grouped_back, input_rows), axis=2))
        input_gradient = jnp.einsum('uomb,muoz->buz', decay_kernel, grouped_gradient)
        input_gradient = input_gradient + lax.optimization_barrier(jnp.sum(grouped_fade * jnp.einsum('sgn,grnp->sgrp', write_rows, grouped_back), axis=2))
        return (readout_gradient.astype(jnp.bfloat16), write_gradient.astype(jnp.bfloat16), input_gradient.astype(jnp.bfloat16))
    readout_gradient, write_gradient, input_gradient = lax.map(final_grads, (block_ids, carry_in, carry_back))
    grad_gain = lax.optimization_barrier(jnp.sum(gain_terms, axis=0)) / SEGMENT_SPAN
    return (readout_gradient.reshape(SEGMENT_SPAN, ATTENTION_LANES, STATE_SIZE), write_gradient.reshape(SEGMENT_SPAN, KV_HEADS, STATE_SIZE), input_gradient.reshape(SEGMENT_SPAN, KV_HEADS, HEAD_SIZE), grad_gain)
```

```python
import functools
import math

import jax
import jax.numpy as jnp
from jax import lax
from jax.experimental import pallas as pl
from jax.experimental.pallas import tpu as pltpu
from jax.sharding import PartitionSpec as P

EPSILON = 1e-05
STUDENT_FLOOR = 1.0
HIDDEN = -1e30
LANES = 128
F32 = jnp.float32
BF16 = jnp.bfloat16
MESH = pl.DeviceIdType.MESH
WRITE, INPUT, KEY, VALUE = range(4)
ARRAYS = 4


def nn(a, b):
    return jnp.dot(a, b, preferred_element_type=F32)


def nt(a, b):
    return lax.dot_general(a, b, (((1,), (1,)), ((), ())), preferred_element_type=F32)


def wide(column, width):
    return column if width == LANES else jnp.concatenate([column] * (width // LANES), axis=1)


def column_of(row):
    return jnp.broadcast_to(row, (LANES, row.shape[1])).T


def kernel(
    n, reach,
    q_ref, c_ref, pack_ref, decay_ref, pos_ref, gain_ref,
    readout_ref, write_ref, input_ref, gain_out_ref,
    halo, own_tail, own_decay, own_rows, halo_rows, level, head_rows, faded_tail, halo_wt,
    c_t, fade, kern, intra, accum, best, head_col, bias,
    own_back, send_back, recv_back, write_t, input_t, gain_sum, gain_slots,
    halo_send, halo_recv, back_send, back_recv, gain_send, gain_recv,
):
    heads, tokens, width = q_ref.shape
    groups = pack_ref.shape[1]
    repeat = heads // groups
    me = lax.axis_index("ctx")
    right, left = me + 1, me - 1

    barrier = pltpu.get_barrier_semaphore()
    for step in range(1, n):
        pl.semaphore_signal(
            barrier, inc=1, device_id={"ctx": lax.rem(me + step, n)}, device_id_type=MESH
        )
    pl.semaphore_wait(barrier, n - 1)

    def shard_copy(hop, part):
        if part == ARRAYS:
            src = own_rows if hop == 1 else halo_rows.at[hop - 2]
            dst = halo_rows.at[hop - 1]
        else:
            src = pack_ref.at[part] if hop == 1 else halo.at[hop - 2, part]
            dst = halo.at[hop - 1, part]
        return pltpu.make_async_remote_copy(
            src_ref=src, dst_ref=dst,
            send_sem=halo_send.at[hop - 1, part], recv_sem=halo_recv.at[hop - 1, part],
            device_id={"ctx": right}, device_id_type=MESH,
        )

    def sends(hop):
        return (me - (hop - 1) >= 0) & (right < n)

    def send_shard(hop, part):
        @pl.when(sends(hop))
        def _():
            shard_copy(hop, part).start()

    def take_shard(hop, part):
        @pl.when(me - hop >= 0)
        def _():
            shard_copy(hop, part).wait_recv()

    for part in range(ARRAYS):
        send_shard(1, part)

    for hop in range(1, reach + 1):
        @pl.when(me - hop < 0)
        def _():
            halo[hop - 1] = jnp.zeros(halo.shape[1:], halo.dtype)
            halo_rows[hop - 1] = jnp.zeros(halo_rows.shape[1:], F32)

    @pl.when(me == n - 1)
    def _():
        recv_back[...] = jnp.zeros(recv_back.shape, recv_back.dtype)

    pos_row = pos_ref[...].astype(F32)
    pos_last = pos_row[:, tokens - 1 :]
    token_row = lax.broadcasted_iota(jnp.int32, (1, tokens), 1).astype(F32)
    row_id = lax.broadcasted_iota(jnp.int32, (tokens, tokens), 0)
    col_id = lax.broadcasted_iota(jnp.int32, (tokens, tokens), 1)
    upper = jnp.where(row_id <= col_id, 1.0, 0.0).astype(F32)
    level[...] = lax.dot_general(
        decay_ref[...], upper, (((0,), (0,)), ((), ())),
        precision=lax.Precision.HIGHEST, preferred_element_type=F32,
    )
    levels = level[...]
    last = levels[:, tokens - 1 :]
    own_tail[...] = jnp.where(
        token_row >= tokens - 1 - pos_last, jnp.exp(last - levels), 0.0
    )
    own_decay[...] = jnp.broadcast_to(
        jnp.where(pos_last > tokens - 1, jnp.exp(last), 0.0), (heads, LANES)
    )
    own_rows[:, :tokens] = own_tail[...]
    own_rows[:, tokens:] = own_decay[...]
    send_shard(1, ARRAYS)
    head_rows[...] = jnp.where(pos_row > token_row, jnp.exp(levels), 0.0)
    pos_col = column_of(pos_row)
    pos_wide = wide(pos_col, tokens)
    apart = (row_id - col_id).astype(F32)
    bias[0] = jnp.where((apart >= 0) & (apart <= pos_wide), 0.0, HIDDEN)
    for hop in range(1, reach + 1):
        bias[hop] = jnp.where(apart + hop * tokens <= pos_wide, 0.0, HIDDEN)
    head_mask = pos_col > lax.broadcasted_iota(jnp.int32, (tokens, LANES), 0).astype(F32)
    head_mask = jnp.where(head_mask, 1.0, 0.0)
    for g in range(groups):
        write_t[g] = jnp.zeros(write_t.shape[1:], F32)
        input_t[g] = jnp.zeros(input_t.shape[1:], F32)
    score_scale = math.log2(math.e) / math.sqrt(width)

    def local_part(h, _):
        g = h // repeat
        c = c_ref[h]
        level_row = level[pl.ds(h, 1), :]
        level_col = column_of(level_row)
        head_col[h] = jnp.exp(level_col) * head_mask
        faded = jnp.exp(wide(level_col, tokens) - level_row + bias[0])
        fade[h] = faded
        within = (faded * nt(c, pack_ref[WRITE, g])).astype(BF16)
        kern[h] = within
        intra[h] = nn(within, pack_ref[INPUT, g])
        scores = nt(q_ref[h], pack_ref[KEY, g]) * score_scale + bias[0]
        top = jnp.max(scores, axis=1, keepdims=True)
        weights = jnp.exp2(scores - top).astype(BF16)
        accum[h] = nn(weights, pack_ref[VALUE, g])
        best[h] = jnp.broadcast_to(top, (tokens, LANES))
        c_t[h] = c.T
        return 0

    lax.fori_loop(0, heads, local_part, 0)

    for hop in range(1, reach + 1):
        for part in range(ARRAYS + 1):
            take_shard(hop, part)
            if hop < reach:
                send_shard(hop + 1, part)
    running = jnp.ones((heads, 1), F32)
    for hop in range(1, reach + 1):
        faded_tail[hop - 1] = halo_rows[hop - 1, :, :tokens] * running
        running = running * halo_rows[hop - 1, :, tokens : tokens + 1]
        for g in range(groups):
            halo_wt[hop - 1, g] = halo[hop - 1, WRITE, g].T

    def back_copy(h):
        return pltpu.make_async_remote_copy(
            src_ref=send_back.at[h], dst_ref=recv_back.at[h],
            send_sem=back_send.at[h], recv_sem=back_recv.at[h],
            device_id={"ctx": left}, device_id_type=MESH,
        )

    def chain(h):
        @pl.when(me < n - 1)
        def _():
            back_copy(h).wait_recv()

        @pl.when(me > 0)
        def _():
            block_decay = own_decay[pl.ds(h, 1), :]
            send_back[h] = (own_back[h] + block_decay * recv_back[h].astype(F32)).astype(BF16)
            back_copy(h).start()

    def main_part(h, _):
        g = h // repeat
        q = q_ref[h]
        c = c_ref[h]
        gain = gain_ref[pl.ds(h, 1), :]
        scores = [
            nt(q, halo[hop, KEY, g]) * score_scale + bias[hop + 1] for hop in range(reach)
        ]
        old_top = best[h]
        top = functools.reduce(jnp.maximum, scores)
        top = jnp.maximum(jnp.max(top, axis=1, keepdims=True), old_top)
        total = accum[h] * jnp.exp2(old_top - top)
        for hop in range(reach):
            weights = jnp.exp2(scores[hop] - wide(top, tokens)).astype(BF16)
            total += nn(weights, halo[hop, VALUE, g])
        target = total * lax.rsqrt(jnp.mean(total * total, axis=1, keepdims=True) + EPSILON)
        target = target.astype(BF16).astype(F32)
        carry = jnp.zeros((c.shape[1], width), F32)
        for hop in range(reach):
            scaled = halo_wt[hop, g].astype(F32) * faded_tail[hop, pl.ds(h, 1), :]
            carry += nn(scaled.astype(BF16), halo[hop, INPUT, g])
        carry_low = carry.astype(BF16)
        head_fade = head_col[h]
        mixer = intra[h] + head_fade * nn(c, carry_low)
        inverse = lax.rsqrt(jnp.mean(mixer * mixer, axis=1, keepdims=True) + STUDENT_FLOOR)
        normed = mixer * inverse
        residual = normed * gain - target
        gain_sum[pl.ds(h, 1), :] = jnp.sum(residual * normed, axis=0, keepdims=True)
        slope = residual * gain
        slope = (slope - normed * jnp.mean(slope * normed, axis=1, keepdims=True)) * inverse
        grad = slope.astype(BF16)
        faded_c = (c_t[h].astype(F32) * head_rows[pl.ds(h, 1), :]).astype(BF16)
        own_back[h] = nn(faded_c, grad)
        grad_kernel = (fade[h] * nt(grad, pack_ref[INPUT, g])).astype(BF16)
        readout = nn(grad_kernel, pack_ref[WRITE, g]) + head_fade * nt(grad, carry_low)
        readout_ref[h] = readout.astype(BF16)
        write_t[g] += nn(c_t[h], grad_kernel)
        input_t[g] += nn(grad.T, kern[h])

        @pl.when(h > 0)
        def _():
            chain(h - 1)

        return 0

    lax.fori_loop(0, heads, main_part, 0)
    chain(heads - 1)

    def gain_copy(step):
        return pltpu.make_async_remote_copy(
            src_ref=gain_sum, dst_ref=gain_slots.at[step - 1],
            send_sem=gain_send.at[step - 1], recv_sem=gain_recv.at[step - 1],
            device_id={"ctx": lax.rem(me + step, n)}, device_id_type=MESH,
        )

    for step in range(1, n):
        gain_copy(step).start()

    def tail_part(h, _):
        g = h // repeat
        tail = own_tail[pl.ds(h, 1), :]
        back = recv_back[h]
        write_t[g] += tail * nt(back, pack_ref[INPUT, g])
        input_t[g] += tail * nt(back.T, pack_ref[WRITE, g])
        return 0

    lax.fori_loop(0, heads, tail_part, 0)
    for g in range(groups):
        write_ref[g] = write_t[g].T.astype(BF16)
        input_ref[g] = input_t[g].T.astype(BF16)

    total_gain = gain_sum[...]
    for step in range(1, n):
        gain_copy(step).wait_recv()
        total_gain += gain_slots[step - 1]
    gain_out_ref[...] = total_gain * (1.0 / (tokens * n))
    for step in range(1, n):
        gain_copy(step).wait_send()
    for hop in range(1, reach + 1):
        @pl.when(sends(hop))
        def _():
            for part in range(ARRAYS + 1):
                shard_copy(hop, part).wait_send()

    @pl.when(me > 0)
    def _():
        def drain(h, _):
            back_copy(h).wait_send()
            return 0

        lax.fori_loop(0, heads, drain, 0)


def body(queries, keys, values, doc_pos, log_decay, student_c, student_write, student_input, gain):
    tokens, heads, width = queries.shape
    groups = keys.shape[1]
    state = student_c.shape[2]
    n = lax.axis_size("ctx")
    reach = max(1, n // 2)
    pack = jnp.stack([student_write, student_input, keys, values]).transpose(0, 2, 1, 3)
    vmem = pl.BlockSpec(memory_space=pltpu.VMEM)
    rows = tokens + LANES
    readout, write, inputs, gain_grad = pl.pallas_call(
        functools.partial(kernel, n, reach),
        out_shape=(
            jax.ShapeDtypeStruct((heads, tokens, state), BF16),
            jax.ShapeDtypeStruct((groups, tokens, state), BF16),
            jax.ShapeDtypeStruct((groups, tokens, width), BF16),
            jax.ShapeDtypeStruct((heads, width), F32),
        ),
        in_specs=[vmem] * 6,
        out_specs=(vmem,) * 4,
        scratch_shapes=[
            pltpu.VMEM((reach, ARRAYS, groups, tokens, width), BF16),
            pltpu.VMEM((heads, tokens), F32),
            pltpu.VMEM((heads, LANES), F32),
            pltpu.VMEM((heads, rows), F32),
            pltpu.VMEM((reach, heads, rows), F32),
            pltpu.VMEM((heads, tokens), F32),
            pltpu.VMEM((heads, tokens), F32),
            pltpu.VMEM((reach, heads, tokens), F32),
            pltpu.VMEM((reach, groups, state, tokens), BF16),
            pltpu.VMEM((heads, state, tokens), BF16),
            pltpu.VMEM((heads, tokens, tokens), F32),
            pltpu.VMEM((heads, tokens, tokens), BF16),
            pltpu.VMEM((heads, tokens, width), F32),
            pltpu.VMEM((heads, tokens, width), F32),
            pltpu.VMEM((heads, tokens, LANES), F32),
            pltpu.VMEM((heads, tokens, LANES), F32),
            pltpu.VMEM((reach + 1, tokens, tokens), F32),
            pltpu.VMEM((heads, state, width), F32),
            pltpu.VMEM((heads, state, width), BF16),
            pltpu.VMEM((heads, state, width), BF16),
            pltpu.VMEM((groups, state, tokens), F32),
            pltpu.VMEM((groups, width, tokens), F32),
            pltpu.VMEM((heads, width), F32),
            pltpu.VMEM((n - 1, heads, width), F32),
            pltpu.SemaphoreType.DMA((reach, ARRAYS + 1)),
            pltpu.SemaphoreType.DMA((reach, ARRAYS + 1)),
            pltpu.SemaphoreType.DMA((heads,)),
            pltpu.SemaphoreType.DMA((heads,)),
            pltpu.SemaphoreType.DMA((n - 1,)),
            pltpu.SemaphoreType.DMA((n - 1,)),
        ],
        compiler_params=pltpu.CompilerParams(
            collective_id=0, has_side_effects=True, vmem_limit_bytes=48 * 2**20
        ),
    )(
        queries.transpose(1, 0, 2),
        student_c.transpose(1, 0, 2),
        pack,
        log_decay,
        doc_pos.reshape(1, tokens),
        gain,
    )
    return (
        readout.transpose(1, 0, 2),
        write.transpose(1, 0, 2),
        inputs.transpose(1, 0, 2),
        gain_grad,
    )


def solution(mesh):
    tokens = P(("groups", "ctx"), "tp", None)
    return jax.shard_map(
        body,
        mesh=mesh,
        in_specs=(
            tokens, tokens, tokens, P(("groups", "ctx")), P(("groups", "ctx"), "tp"),
            tokens, tokens, tokens, P("tp", None),
        ),
        out_specs=(tokens, tokens, tokens, P(("groups", "tp"), None)),
        check_vma=False,
    )
```

```python
import functools
import math

import jax
import jax.numpy as jnp
from jax import lax
from jax.experimental import pallas as pl
from jax.experimental.pallas import tpu as pltpu
from jax.sharding import PartitionSpec as P

EPSILON = 1e-05
STUDENT_FLOOR = 1.0
HIDDEN = -1e30
LANES = 128
F32 = jnp.float32
BF16 = jnp.bfloat16
MESH = pl.DeviceIdType.MESH
WRITE, INPUT, KEY, VALUE = range(4)
ARRAYS = 4
TOGETHER = 4


def nn(a, b):
    return jnp.dot(a, b, preferred_element_type=F32)


def nt(a, b):
    return lax.dot_general(a, b, (((1,), (1,)), ((), ())), preferred_element_type=F32)


def wide(column, width):
    return column if width == LANES else jnp.concatenate([column] * (width // LANES), axis=1)


def column_of(row):
    return jnp.broadcast_to(row, (LANES, row.shape[1])).T


def kernel(
    n, reach,
    q_ref, c_ref, pack_ref, decay_ref, pos_ref, gain_ref,
    readout_ref, write_ref, input_ref, gain_out_ref,
    halo, own_tail, own_decay, own_rows, halo_rows, level, head_rows, faded_tail, halo_wt,
    c_t, fade, kern, intra, accum, best, head_col, bias,
    own_back, send_back, recv_back, write_t, input_t, gain_sum, gain_slots,
    halo_send, halo_recv, back_send, back_recv, gain_send, gain_recv,
):
    heads, tokens, width = q_ref.shape
    groups = pack_ref.shape[0]
    repeat = heads // groups
    me = lax.axis_index("ctx")
    right, left = me + 1, me - 1

    barrier = pltpu.get_barrier_semaphore()
    for step in range(1, n):
        pl.semaphore_signal(
            barrier, inc=1, device_id={"ctx": lax.rem(me + step, n)}, device_id_type=MESH
        )
    pl.semaphore_wait(barrier, n - 1)

    def shard_copy(hop, part):
        if part == groups:
            src = own_rows if hop == 1 else halo_rows.at[hop - 2]
            dst = halo_rows.at[hop - 1]
        else:
            src = pack_ref.at[part] if hop == 1 else halo.at[hop - 2, part]
            dst = halo.at[hop - 1, part]
        return pltpu.make_async_remote_copy(
            src_ref=src, dst_ref=dst,
            send_sem=halo_send.at[hop - 1, part], recv_sem=halo_recv.at[hop - 1, part],
            device_id={"ctx": right}, device_id_type=MESH,
        )

    def sends(hop):
        return (me - (hop - 1) >= 0) & (right < n)

    def send_shard(hop, part):
        @pl.when(sends(hop))
        def _():
            shard_copy(hop, part).start()

    def take_shard(hop, part):
        @pl.when(me - hop >= 0)
        def _():
            shard_copy(hop, part).wait_recv()

    send_shard(1, 0)

    for hop in range(1, reach + 1):
        @pl.when(me - hop < 0)
        def _():
            halo[hop - 1] = jnp.zeros(halo.shape[1:], halo.dtype)
            halo_rows[hop - 1] = jnp.zeros(halo_rows.shape[1:], F32)

    @pl.when(me == n - 1)
    def _():
        recv_back[...] = jnp.zeros(recv_back.shape, recv_back.dtype)

    pos_row = pos_ref[...].astype(F32)
    pos_last = pos_row[:, tokens - 1 :]
    token_row = lax.broadcasted_iota(jnp.int32, (1, tokens), 1).astype(F32)
    row_id = lax.broadcasted_iota(jnp.int32, (tokens, tokens), 0)
    col_id = lax.broadcasted_iota(jnp.int32, (tokens, tokens), 1)
    upper = jnp.where(row_id <= col_id, 1.0, 0.0).astype(F32)
    level[...] = jnp.dot(
        decay_ref[...], upper, precision=lax.Precision.HIGHEST, preferred_element_type=F32
    )
    levels = level[...]
    last = levels[:, tokens - 1 :]
    own_tail[...] = jnp.where(
        token_row >= tokens - 1 - pos_last, jnp.exp(last - levels), 0.0
    )
    own_decay[...] = jnp.broadcast_to(
        jnp.where(pos_last > tokens - 1, jnp.exp(last), 0.0), (heads, LANES)
    )
    own_rows[:, :tokens] = own_tail[...]
    own_rows[:, tokens:] = own_decay[...]
    send_shard(1, groups)
    head_rows[...] = jnp.where(pos_row > token_row, jnp.exp(levels), 0.0)
    pos_col = column_of(pos_row)
    pos_wide = wide(pos_col, tokens)
    apart = (row_id - col_id).astype(F32)
    bias[0] = jnp.where((apart >= 0) & (apart <= pos_wide), 0.0, HIDDEN)
    for hop in range(1, reach + 1):
        bias[hop] = jnp.where(apart + hop * tokens <= pos_wide, 0.0, HIDDEN)
    head_mask = pos_col > lax.broadcasted_iota(jnp.int32, (tokens, LANES), 0).astype(F32)
    head_mask = jnp.where(head_mask, 1.0, 0.0)
    for g in range(groups):
        write_t[g] = jnp.zeros(write_t.shape[1:], F32)
        input_t[g] = jnp.zeros(input_t.shape[1:], F32)
    score_scale = math.log2(math.e) / math.sqrt(width)

    def local_part(h):
        g = h // repeat
        c = c_ref[h]
        level_row = level[pl.ds(h, 1), :]
        level_col = column_of(level_row)
        head_col[h] = jnp.exp(level_col) * head_mask
        faded = jnp.exp(wide(level_col, tokens) - level_row + bias[0])
        fade[h] = faded
        within = (faded * nt(c, pack_ref[g, WRITE])).astype(BF16)
        kern[h] = within
        intra[h] = nn(within, pack_ref[g, INPUT])
        scores = nt(q_ref[h], pack_ref[g, KEY]) * score_scale + bias[0]
        top = jnp.max(scores, axis=1, keepdims=True)
        weights = jnp.exp2(scores - top).astype(BF16)
        accum[h] = nn(weights, pack_ref[g, VALUE])
        best[h] = jnp.broadcast_to(top, (tokens, LANES))
        c_t[h] = c.T

    def arrive(group, hop):
        parts = (group, groups) if group == 0 else (group,)
        for part in parts:
            take_shard(hop, part)
            if hop < reach:
                send_shard(hop + 1, part)
        if hop == 1 and group + 1 < groups:
            send_shard(1, group + 1)

    def ready(group):
        for hop in range(2, reach + 1):
            arrive(group, hop)
        if group == 0:
            running = jnp.ones((heads, 1), F32)
            for hop in range(1, reach + 1):
                faded_tail[hop - 1] = halo_rows[hop - 1, :, :tokens] * running
                running = running * halo_rows[hop - 1, :, tokens : tokens + 1]
        for hop in range(1, reach + 1):
            halo_wt[hop - 1, group] = halo[hop - 1, group, WRITE].T

    together = math.gcd(repeat, TOGETHER)

    def per_heads(first, past, part, after=None):
        def step(index, _):
            for offset in range(together):
                part(index * together + offset)
            if after is not None:
                after(index)
            return 0

        lax.fori_loop(first // together, past // together, step, 0)

    per_heads(0, repeat, local_part)
    arrive(0, 1)
    if groups > 1:
        per_heads(repeat, heads, local_part)
    ready(0)

    def back_copy(h):
        return pltpu.make_async_remote_copy(
            src_ref=send_back.at[h], dst_ref=recv_back.at[h],
            send_sem=back_send.at[h], recv_sem=back_recv.at[h],
            device_id={"ctx": left}, device_id_type=MESH,
        )

    def chain(h):
        @pl.when(me < n - 1)
        def _():
            back_copy(h).wait_recv()

        @pl.when(me > 0)
        def _():
            block_decay = own_decay[pl.ds(h, 1), :]
            send_back[h] = (own_back[h] + block_decay * recv_back[h].astype(F32)).astype(BF16)
            back_copy(h).start()

    def main_part(h):
        g = h // repeat
        q = q_ref[h]
        c = c_ref[h]
        gain = gain_ref[pl.ds(h, 1), :]
        scores = [
            nt(q, halo[hop, g, KEY]) * score_scale + bias[hop + 1] for hop in range(reach)
        ]
        old_top = best[h]
        top = functools.reduce(jnp.maximum, scores)
        top = jnp.maximum(jnp.max(top, axis=1, keepdims=True), old_top)
        total = accum[h] * jnp.exp2(old_top - top)
        for hop in range(reach):
            weights = jnp.exp2(scores[hop] - wide(top, tokens)).astype(BF16)
            total += nn(weights, halo[hop, g, VALUE])
        target = total * lax.rsqrt(jnp.mean(total * total, axis=1, keepdims=True) + EPSILON)
        target = target.astype(BF16).astype(F32)
        carry = jnp.zeros((c.shape[1], width), F32)
        for hop in range(reach):
            scaled = halo_wt[hop, g].astype(F32) * faded_tail[hop, pl.ds(h, 1), :]
            carry += nn(scaled.astype(BF16), halo[hop, g, INPUT])
        carry_low = carry.astype(BF16)
        head_fade = head_col[h]
        mixer = intra[h] + head_fade * nn(c, carry_low)
        inverse = lax.rsqrt(jnp.mean(mixer * mixer, axis=1, keepdims=True) + STUDENT_FLOOR)
        normed = mixer * inverse
        residual = normed * gain - target
        gain_sum[pl.ds(h, 1), :] = jnp.sum(residual * normed, axis=0, keepdims=True)
        slope = residual * gain
        slope = (slope - normed * jnp.mean(slope * normed, axis=1, keepdims=True)) * inverse
        grad = slope.astype(BF16)
        faded_c = (c_t[h].astype(F32) * head_rows[pl.ds(h, 1), :]).astype(BF16)
        own_back[h] = nn(faded_c, grad)
        grad_kernel = (fade[h] * nt(grad, pack_ref[g, INPUT])).astype(BF16)
        readout = nn(grad_kernel, pack_ref[g, WRITE]) + head_fade * nt(grad, carry_low)
        readout_ref[h] = readout.astype(BF16)
        write_t[g] += nn(c_t[h], grad_kernel)
        input_t[g] += nn(grad.T, kern[h])

    behind = n - 1 - me
    steps = heads // together

    def hand_on(index):
        for offset in range(together):
            chain(index * together + offset)

    def hand_on_late(index):
        @pl.when(index - behind >= 0)
        def _():
            hand_on(index - behind)

    half = repeat // together // 2 * together
    for group in range(groups):
        first = group * repeat
        if group + 1 < groups:
            per_heads(first, first + half, main_part, hand_on_late)
            arrive(group + 1, 1)
            per_heads(first + half, first + repeat, main_part, hand_on_late)
            ready(group + 1)
        else:
            per_heads(first, first + repeat, main_part, hand_on_late)

    def gain_copy(step):
        return pltpu.make_async_remote_copy(
            src_ref=gain_sum, dst_ref=gain_slots.at[step - 1],
            send_sem=gain_send.at[step - 1], recv_sem=gain_recv.at[step - 1],
            device_id={"ctx": lax.rem(me + step, n)}, device_id_type=MESH,
        )

    for step in range(1, n):
        gain_copy(step).start()

    def tail_part(h):
        g = h // repeat
        tail = own_tail[pl.ds(h, 1), :]
        back = recv_back[h]
        write_t[g] += tail * nt(back, pack_ref[g, INPUT])
        input_t[g] += tail * nt(back.T, pack_ref[g, WRITE])

    def tail_step(index, _):
        @pl.when(index + behind >= steps)
        def _():
            hand_on(index)

        for offset in range(together):
            tail_part(index * together + offset)
        return 0

    lax.fori_loop(0, steps, tail_step, 0)
    for g in range(groups):
        write_ref[g] = write_t[g].T.astype(BF16)
        input_ref[g] = input_t[g].T.astype(BF16)

    total_gain = gain_sum[...]
    for step in range(1, n):
        gain_copy(step).wait_recv()
        total_gain += gain_slots[step - 1]
    gain_out_ref[...] = total_gain * (1.0 / (tokens * n))
    for step in range(1, n):
        gain_copy(step).wait_send()
    for hop in range(1, reach + 1):
        @pl.when(sends(hop))
        def _():
            for part in range(groups + 1):
                shard_copy(hop, part).wait_send()

    @pl.when(me > 0)
    def _():
        def drain(h, _):
            back_copy(h).wait_send()
            return 0

        lax.fori_loop(0, heads, drain, 0)


def body(queries, keys, values, doc_pos, log_decay, student_c, student_write, student_input, gain):
    tokens, heads, width = queries.shape
    groups = keys.shape[1]
    state = student_c.shape[2]
    n = lax.axis_size("ctx")
    reach = max(1, n // 2)
    pack = jnp.stack([student_write, student_input, keys, values]).transpose(2, 0, 1, 3)
    vmem = pl.BlockSpec(memory_space=pltpu.VMEM)
    rows = tokens + LANES
    readout, write, inputs, gain_grad = pl.pallas_call(
        functools.partial(kernel, n, reach),
        out_shape=(
            jax.ShapeDtypeStruct((heads, tokens, state), BF16),
            jax.ShapeDtypeStruct((groups, tokens, state), BF16),
            jax.ShapeDtypeStruct((groups, tokens, width), BF16),
            jax.ShapeDtypeStruct((heads, width), F32),
        ),
        in_specs=[vmem] * 6,
        out_specs=(vmem,) * 4,
        scratch_shapes=[
            pltpu.VMEM((reach, groups, ARRAYS, tokens, width), BF16),
            pltpu.VMEM((heads, tokens), F32),
            pltpu.VMEM((heads, LANES), F32),
            pltpu.VMEM((heads, rows), F32),
            pltpu.VMEM((reach, heads, rows), F32),
            pltpu.VMEM((heads, tokens), F32),
            pltpu.VMEM((heads, tokens), F32),
            pltpu.VMEM((reach, heads, tokens), F32),
            pltpu.VMEM((reach, groups, state, tokens), BF16),
            pltpu.VMEM((heads, state, tokens), BF16),
            pltpu.VMEM((heads, tokens, tokens), F32),
            pltpu.VMEM((heads, tokens, tokens), BF16),
            pltpu.VMEM((heads, tokens, width), F32),
            pltpu.VMEM((heads, tokens, width), F32),
            pltpu.VMEM((heads, tokens, LANES), F32),
            pltpu.VMEM((heads, tokens, LANES), F32),
            pltpu.VMEM((reach + 1, tokens, tokens), F32),
            pltpu.VMEM((heads, state, width), F32),
            pltpu.VMEM((heads, state, width), BF16),
            pltpu.VMEM((heads, state, width), BF16),
            pltpu.VMEM((groups, state, tokens), F32),
            pltpu.VMEM((groups, width, tokens), F32),
            pltpu.VMEM((heads, width), F32),
            pltpu.VMEM((n - 1, heads, width), F32),
            pltpu.SemaphoreType.DMA((reach, groups + 1)),
            pltpu.SemaphoreType.DMA((reach, groups + 1)),
            pltpu.SemaphoreType.DMA((heads,)),
            pltpu.SemaphoreType.DMA((heads,)),
            pltpu.SemaphoreType.DMA((n - 1,)),
            pltpu.SemaphoreType.DMA((n - 1,)),
        ],
        compiler_params=pltpu.CompilerParams(
            collective_id=0, has_side_effects=True, vmem_limit_bytes=48 * 2**20
        ),
    )(
        queries.transpose(1, 0, 2),
        student_c.transpose(1, 0, 2),
        pack,
        log_decay.T,
        doc_pos.reshape(1, tokens),
        gain,
    )
    return (
        readout.transpose(1, 0, 2),
        write.transpose(1, 0, 2),
        inputs.transpose(1, 0, 2),
        gain_grad,
    )


def solution(mesh):
    tokens = P(("groups", "ctx"), "tp", None)
    return jax.shard_map(
        body,
        mesh=mesh,
        in_specs=(
            tokens, tokens, tokens, P(("groups", "ctx")), P(("groups", "ctx"), "tp"),
            tokens, tokens, tokens, P("tp", None),
        ),
        out_specs=(tokens, tokens, tokens, P(("groups", "tp"), None)),
        check_vma=False,
    )
```

```python
import functools
import math

import jax
import jax.numpy as jnp
from jax import lax
from jax.experimental import pallas as pl
from jax.experimental.pallas import tpu as pltpu
from jax.sharding import PartitionSpec as P

EPSILON = 1e-05
STUDENT_FLOOR = 1.0
HIDDEN = -1e30
LANES = 128
F32 = jnp.float32
BF16 = jnp.bfloat16
MESH = pl.DeviceIdType.MESH
WRITE, INPUT, KEY, VALUE = range(4)
ARRAYS = 4
TOGETHER = 4
CHUNK = 64


def nn(a, b):
    return jnp.dot(a, b, preferred_element_type=F32)


def nt(a, b):
    return lax.dot_general(a, b, (((1,), (1,)), ((), ())), preferred_element_type=F32)


def wide(column, width):
    return column if width == LANES else jnp.concatenate([column] * (width // LANES), axis=1)


def column_of(row):
    return jnp.broadcast_to(row, (LANES, row.shape[1])).T


def kernel(
    n, reach,
    q_rows, c_rows, pack_ref, decay_ref, pos_ref, gain_ref,
    readout_rows, write_ref, input_ref, gain_out_ref,
    q_ref, c_ref, readout_ref, halo, own_tail, own_decay, own_rows, halo_rows, level, head_rows, faded_tail, halo_wt,
    c_t, fade, kern, intra, accum, best, head_col, bias,
    own_back, send_back, recv_back, write_t, input_t, gain_sum, gain_slots,
    halo_send, halo_recv, back_send, back_recv, gain_send, gain_recv,
):
    tokens, heads, width = q_rows.shape
    groups = pack_ref.shape[0]
    repeat = heads // groups
    me = lax.axis_index("ctx")
    right, left = me + 1, me - 1

    barrier = pltpu.get_barrier_semaphore()
    for step in range(1, n):
        pl.semaphore_signal(
            barrier, inc=1, device_id={"ctx": lax.rem(me + step, n)}, device_id_type=MESH
        )
    pl.semaphore_wait(barrier, n - 1)

    def shard_copy(hop, part):
        if part == groups:
            src = own_rows if hop == 1 else halo_rows.at[hop - 2]
            dst = halo_rows.at[hop - 1]
        else:
            src = pack_ref.at[part] if hop == 1 else halo.at[hop - 2, part]
            dst = halo.at[hop - 1, part]
        return pltpu.make_async_remote_copy(
            src_ref=src, dst_ref=dst,
            send_sem=halo_send.at[hop - 1, part], recv_sem=halo_recv.at[hop - 1, part],
            device_id={"ctx": right}, device_id_type=MESH,
        )

    def sends(hop):
        return (me - (hop - 1) >= 0) & (right < n)

    def send_shard(hop, part):
        @pl.when(sends(hop))
        def _():
            shard_copy(hop, part).start()

    def take_shard(hop, part):
        @pl.when(me - hop >= 0)
        def _():
            shard_copy(hop, part).wait_recv()

    send_shard(1, 0)

    for hop in range(1, reach + 1):
        @pl.when(me - hop < 0)
        def _():
            halo[hop - 1] = jnp.zeros(halo.shape[1:], halo.dtype)
            halo_rows[hop - 1] = jnp.zeros(halo_rows.shape[1:], F32)

    @pl.when(me == n - 1)
    def _():
        recv_back[...] = jnp.zeros(recv_back.shape, recv_back.dtype)

    pos_row = pos_ref[...].astype(F32)
    pos_last = pos_row[:, tokens - 1 :]
    token_row = lax.broadcasted_iota(jnp.int32, (1, tokens), 1).astype(F32)
    row_id = lax.broadcasted_iota(jnp.int32, (tokens, tokens), 0)
    col_id = lax.broadcasted_iota(jnp.int32, (tokens, tokens), 1)
    upper = jnp.where(row_id <= col_id, 1.0, 0.0).astype(F32)
    level[...] = jnp.dot(
        decay_ref[...], upper, precision=lax.Precision.HIGHEST, preferred_element_type=F32
    )
    levels = level[...]
    last = levels[:, tokens - 1 :]
    own_tail[...] = jnp.where(
        token_row >= tokens - 1 - pos_last, jnp.exp(last - levels), 0.0
    )
    own_decay[...] = jnp.broadcast_to(
        jnp.where(pos_last > tokens - 1, jnp.exp(last), 0.0), (heads, LANES)
    )
    own_rows[:, :tokens] = own_tail[...]
    own_rows[:, tokens:] = own_decay[...]
    send_shard(1, groups)
    head_rows[...] = jnp.where(pos_row > token_row, jnp.exp(levels), 0.0)
    pos_col = column_of(pos_row)
    pos_wide = wide(pos_col, tokens)
    apart = (row_id - col_id).astype(F32)
    bias[0] = jnp.where((apart >= 0) & (apart <= pos_wide), 0.0, HIDDEN)
    for hop in range(1, reach + 1):
        bias[hop] = jnp.where(apart + hop * tokens <= pos_wide, 0.0, HIDDEN)
    head_mask = pos_col > lax.broadcasted_iota(jnp.int32, (tokens, LANES), 0).astype(F32)
    head_mask = jnp.where(head_mask, 1.0, 0.0)
    for g in range(groups):
        write_t[g] = jnp.zeros(write_t.shape[1:], F32)
        input_t[g] = jnp.zeros(input_t.shape[1:], F32)
    score_scale = math.log2(math.e) / math.sqrt(width)

    def by_head(index, _):
        rows = pl.ds(pl.multiple_of(index * CHUNK, CHUNK), CHUNK)
        q_ref[:, rows, :] = jnp.transpose(q_rows[rows], (1, 0, 2))
        c_ref[:, rows, :] = jnp.transpose(c_rows[rows], (1, 0, 2))
        return 0

    lax.fori_loop(0, tokens // CHUNK, by_head, 0)

    def local_part(h):
        g = h // repeat
        c = c_ref[h]
        level_row = level[pl.ds(h, 1), :]
        level_col = column_of(level_row)
        head_col[h] = jnp.exp(level_col) * head_mask
        faded = jnp.exp(wide(level_col, tokens) - level_row + bias[0])
        fade[h] = faded
        within = (faded * nt(c, pack_ref[g, WRITE])).astype(BF16)
        kern[h] = within
        intra[h] = nn(within, pack_ref[g, INPUT])
        scores = nt(q_ref[h], pack_ref[g, KEY]) * score_scale + bias[0]
        top = jnp.max(scores, axis=1, keepdims=True)
        weights = jnp.exp2(scores - top).astype(BF16)
        accum[h] = nn(weights, pack_ref[g, VALUE])
        best[h] = jnp.broadcast_to(top, (tokens, LANES))
        c_t[h] = c.T

    def arrive(group, hop):
        parts = (group, groups) if group == 0 else (group,)
        for part in parts:
            take_shard(hop, part)
            if hop < reach:
                send_shard(hop + 1, part)
        if hop == 1 and group + 1 < groups:
            send_shard(1, group + 1)

    def ready(group):
        for hop in range(2, reach + 1):
            per_heads(group * repeat, (group + 1) * repeat, early_part(hop - 1))
            arrive(group, hop)
        if group == 0:
            running = jnp.ones((heads, 1), F32)
            for hop in range(1, reach + 1):
                faded_tail[hop - 1] = halo_rows[hop - 1, :, :tokens] * running
                running = running * halo_rows[hop - 1, :, tokens : tokens + 1]
        for hop in range(1, reach + 1):
            halo_wt[hop - 1, group] = halo[hop - 1, group, WRITE].T

    together = math.gcd(repeat, TOGETHER)

    def per_heads(first, past, part, after=None):
        def step(index, _):
            for offset in range(together):
                part(index * together + offset)
            if after is not None:
                after(index)
            return 0

        lax.fori_loop(first // together, past // together, step, 0)

    def back_copy(h):
        return pltpu.make_async_remote_copy(
            src_ref=send_back.at[h], dst_ref=recv_back.at[h],
            send_sem=back_send.at[h], recv_sem=back_recv.at[h],
            device_id={"ctx": left}, device_id_type=MESH,
        )

    def chain(h):
        @pl.when(me < n - 1)
        def _():
            back_copy(h).wait_recv()

        @pl.when(me > 0)
        def _():
            block_decay = own_decay[pl.ds(h, 1), :]
            send_back[h] = (own_back[h] + block_decay * recv_back[h].astype(F32)).astype(BF16)
            back_copy(h).start()

    def attend(h, hop):
        g = h // repeat
        scores = nt(q_ref[h], halo[hop - 1, g, KEY]) * score_scale + bias[hop]
        old_top = best[h]
        top = jnp.maximum(jnp.max(scores, axis=1, keepdims=True), old_top)
        weights = jnp.exp2(scores - wide(top, tokens)).astype(BF16)
        return top, accum[h] * jnp.exp2(old_top - top) + nn(weights, halo[hop - 1, g, VALUE])

    def early_part(hop):
        def part(h):
            best[h], accum[h] = attend(h, hop)

        return part

    def main_part(h):
        g = h // repeat
        c = c_ref[h]
        gain = gain_ref[pl.ds(h, 1), :]
        total = attend(h, reach)[1]
        target = total * lax.rsqrt(jnp.mean(total * total, axis=1, keepdims=True) + EPSILON)
        target = target.astype(BF16).astype(F32)
        carry = jnp.zeros((c.shape[1], width), F32)
        for hop in range(reach):
            scaled = halo_wt[hop, g].astype(F32) * faded_tail[hop, pl.ds(h, 1), :]
            carry += nn(scaled.astype(BF16), halo[hop, g, INPUT])
        carry_low = carry.astype(BF16)
        head_fade = head_col[h]
        mixer = intra[h] + head_fade * nn(c, carry_low)
        inverse = lax.rsqrt(jnp.mean(mixer * mixer, axis=1, keepdims=True) + STUDENT_FLOOR)
        normed = mixer * inverse
        residual = normed * gain - target
        gain_sum[pl.ds(h, 1), :] = jnp.sum(residual * normed, axis=0, keepdims=True)
        slope = residual * gain
        slope = (slope - normed * jnp.mean(slope * normed, axis=1, keepdims=True)) * inverse
        grad = slope.astype(BF16)
        faded_c = (c_t[h].astype(F32) * head_rows[pl.ds(h, 1), :]).astype(BF16)
        own_back[h] = nn(faded_c, grad)
        grad_kernel = (fade[h] * nt(grad, pack_ref[g, INPUT])).astype(BF16)
        readout = nn(grad_kernel, pack_ref[g, WRITE]) + head_fade * nt(grad, carry_low)
        readout_ref[h] = readout.astype(BF16)
        write_t[g] += nn(c_t[h], grad_kernel)
        input_t[g] += nn(grad.T, kern[h])

    behind = n - 1 - me
    steps = heads // together

    def hand_on(index):
        for offset in range(together):
            chain(index * together + offset)

    def hand_on_late(index):
        @pl.when(index - behind >= 0)
        def _():
            hand_on(index - behind)

    half = repeat // together // 2 * together
    per_heads(0, repeat, local_part)
    arrive(0, 1)
    if groups > 1:
        per_heads(repeat, heads, local_part)
    ready(0)
    for group in range(groups):
        first = group * repeat
        if group + 1 < groups:
            per_heads(first, first + half, main_part, hand_on_late)
            arrive(group + 1, 1)
            per_heads(first + half, first + repeat, main_part, hand_on_late)
            ready(group + 1)
        else:
            per_heads(first, first + repeat, main_part, hand_on_late)

    def gain_copy(step):
        return pltpu.make_async_remote_copy(
            src_ref=gain_sum, dst_ref=gain_slots.at[step - 1],
            send_sem=gain_send.at[step - 1], recv_sem=gain_recv.at[step - 1],
            device_id={"ctx": lax.rem(me + step, n)}, device_id_type=MESH,
        )

    for step in range(1, n):
        gain_copy(step).start()

    def tail_part(h):
        g = h // repeat
        tail = own_tail[pl.ds(h, 1), :]
        back = recv_back[h]
        write_t[g] += tail * nt(back, pack_ref[g, INPUT])
        input_t[g] += tail * nt(back.T, pack_ref[g, WRITE])

    def by_token(index, _):
        rows = pl.ds(pl.multiple_of(index * CHUNK, CHUNK), CHUNK)
        readout_rows[rows] = jnp.transpose(readout_ref[:, rows, :], (1, 0, 2))
        return 0

    lax.fori_loop(0, tokens // CHUNK, by_token, 0)

    def tail_step(index, _):
        @pl.when(index + behind >= steps)
        def _():
            hand_on(index)

        for offset in range(together):
            tail_part(index * together + offset)
        return 0

    lax.fori_loop(0, steps, tail_step, 0)
    for g in range(groups):
        write_ref[g] = write_t[g].T.astype(BF16)
        input_ref[g] = input_t[g].T.astype(BF16)

    total_gain = gain_sum[...]
    for step in range(1, n):
        gain_copy(step).wait_recv()
        total_gain += gain_slots[step - 1]
    gain_out_ref[...] = total_gain * (1.0 / (tokens * n))
    for step in range(1, n):
        gain_copy(step).wait_send()
    for hop in range(1, reach + 1):
        @pl.when(sends(hop))
        def _():
            for part in range(groups + 1):
                shard_copy(hop, part).wait_send()

    @pl.when(me > 0)
    def _():
        def drain(h, _):
            back_copy(h).wait_send()
            return 0

        lax.fori_loop(0, heads, drain, 0)


def body(queries, keys, values, doc_pos, log_decay, student_c, student_write, student_input, gain):
    tokens, heads, width = queries.shape
    groups = keys.shape[1]
    state = student_c.shape[2]
    n = lax.axis_size("ctx")
    reach = max(1, n // 2)
    pack = jnp.stack([student_write, student_input, keys, values]).transpose(2, 0, 1, 3)
    vmem = pl.BlockSpec(memory_space=pltpu.VMEM)
    rows = tokens + LANES
    readout, write, inputs, gain_grad = pl.pallas_call(
        functools.partial(kernel, n, reach),
        out_shape=(
            jax.ShapeDtypeStruct((tokens, heads, state), BF16),
            jax.ShapeDtypeStruct((groups, tokens, state), BF16),
            jax.ShapeDtypeStruct((groups, tokens, width), BF16),
            jax.ShapeDtypeStruct((heads, width), F32),
        ),
        in_specs=[vmem] * 6,
        out_specs=(vmem,) * 4,
        scratch_shapes=[
            pltpu.VMEM((heads, tokens, width), BF16),
            pltpu.VMEM((heads, tokens, state), BF16),
            pltpu.VMEM((heads, tokens, state), BF16),
            pltpu.VMEM((reach, groups, ARRAYS, tokens, width), BF16),
            pltpu.VMEM((heads, tokens), F32),
            pltpu.VMEM((heads, LANES), F32),
            pltpu.VMEM((heads, rows), F32),
            pltpu.VMEM((reach, heads, rows), F32),
            pltpu.VMEM((heads, tokens), F32),
            pltpu.VMEM((heads, tokens), F32),
            pltpu.VMEM((reach, heads, tokens), F32),
            pltpu.VMEM((reach, groups, state, tokens), BF16),
            pltpu.VMEM((heads, state, tokens), BF16),
            pltpu.VMEM((heads, tokens, tokens), F32),
            pltpu.VMEM((heads, tokens, tokens), BF16),
            pltpu.VMEM((heads, tokens, width), F32),
            pltpu.VMEM((heads, tokens, width), F32),
            pltpu.VMEM((heads, tokens, LANES), F32),
            pltpu.VMEM((heads, tokens, LANES), F32),
            pltpu.VMEM((reach + 1, tokens, tokens), F32),
            pltpu.VMEM((heads, state, width), F32),
            pltpu.VMEM((heads, state, width), BF16),
            pltpu.VMEM((heads, state, width), BF16),
            pltpu.VMEM((groups, state, tokens), F32),
            pltpu.VMEM((groups, width, tokens), F32),
            pltpu.VMEM((heads, width), F32),
            pltpu.VMEM((n - 1, heads, width), F32),
            pltpu.SemaphoreType.DMA((reach, groups + 1)),
            pltpu.SemaphoreType.DMA((reach, groups + 1)),
            pltpu.SemaphoreType.DMA((heads,)),
            pltpu.SemaphoreType.DMA((heads,)),
            pltpu.SemaphoreType.DMA((n - 1,)),
            pltpu.SemaphoreType.DMA((n - 1,)),
        ],
        compiler_params=pltpu.CompilerParams(
            collective_id=0, has_side_effects=True, vmem_limit_bytes=48 * 2**20
        ),
    )(
        queries,
        student_c,
        pack,
        log_decay.T,
        doc_pos.reshape(1, tokens),
        gain,
    )
    return (
        readout,
        write.transpose(1, 0, 2),
        inputs.transpose(1, 0, 2),
        gain_grad,
    )


def solution(mesh):
    tokens = P(("groups", "ctx"), "tp", None)
    return jax.shard_map(
        body,
        mesh=mesh,
        in_specs=(
            tokens, tokens, tokens, P(("groups", "ctx")), P(("groups", "ctx"), "tp"),
            tokens, tokens, tokens, P("tp", None),
        ),
        out_specs=(tokens, tokens, tokens, P(("groups", "tp"), None)),
        check_vma=False,
    )
```
